32 devices in a mesh: gx: 4 (over y, core), ta: 8 (over z, x).
Axes of the slice: x: 2, y: 2, z: 4, core: 2. Of those that a mesh axis runs over, the one named last changes fastest.
Arguments:
- fine_field: bfloat16 [4, 8, 2048, 384], P('gx', 'ta'), may hold values from -40 to 40
- site_map: int32 [4, 8, 2048], P('gx', 'ta'), may hold values from 0 to 2047, each once within a row
- prolongator: bfloat16 [4, 8, 8, 64, 6144], P('gx', 'ta'), may hold values from -0.119628906 to 0.119628906
- coarse_op: bfloat16 [4, 8, 8, 9, 64, 64], P('gx', 'ta'), may hold values from -0.2 to 1.2
Outputs:
- correction: bfloat16 [4, 8, 2048, 384], P('gx', 'ta')
- coarse_residual: float32 [4, 8, 8, 64, 16], P('gx', 'ta')
- residual_norm: float32 [16], replicated
The draws below stay inside these ranges and needn't reach their ends.
Inputs may be any that keep to these rules, and one draw needn't show every extreme that they name: `site_map`: each slab's row of the map names every storage row once.
All inputs are finite; a program needn't handle non-finite values.
Results may differ from the reference program's by a relative error of at most 0.013.
Values may be sent and summed in bfloat16 or wider, within the bound.
A program may use at most 64 MiB of HBM per device.

```python
import math
import jax
import jax.numpy as jnp
from jax import lax

NC = 64
BLK = 256
SPIN = 24
RHS = 16
XC = 4
YC = 2
Z = 4
T_SIZE = 8


def draw_fine_field(key, part):
    key = jax.random.fold_in(key, 11)
    shape = (Z, T_SIZE, XC * YC * BLK, SPIN * RHS)
    z_ramp = jnp.arange(Z, dtype=jnp.float32) / max(Z - 1, 1)
    t_ramp = jnp.arange(T_SIZE, dtype=jnp.float32) / max(T_SIZE - 1, 1)
    ramp = jnp.exp(math.log(3.0) * z_ramp)[:, None] * jnp.exp(math.log(3.0) * t_ramp)[None, :]
    ramp = ramp[:, :, None, None]
    values = jnp.clip(jax.random.normal(key, shape, jnp.float32), -4.0, 4.0) * ramp
    return values.astype(jnp.bfloat16)


def draw_coarse_op(key, part):
    key = jax.random.fold_in(key, 23)
    shape = (Z, T_SIZE, XC * YC, 9, NC, NC)
    noise = jnp.clip(0.042 * jax.random.normal(key, shape, jnp.float32), -0.195, 0.195)
    selfmask = (jnp.arange(9) == 0).astype(jnp.float32)[:, None, None]
    values = noise + selfmask * jnp.eye(NC, dtype=jnp.float32)[None, :, :]
    return values.astype(jnp.bfloat16)


def shard_levels(key, shape, cuts, low, top_value):
    gain, own = 1.0, jax.random.fold_in(key, 6)
    for axis_at, shards_of in cuts:
        draws = jnp.exp(jax.random.uniform(jax.random.fold_in(own, axis_at), (shards_of,), jnp.float32, low / len(cuts), top_value / len(cuts)))
        gain = gain * jnp.repeat(draws, shape[axis_at] // shards_of).reshape([-1 if axis == axis_at else 1 for axis in range(len(shape))])
    return gain


def bell_draw(key, extent, spread, bound, split=(), held_as=jnp.bfloat16):
    values = jax.random.normal(key, extent, jnp.float32) * spread
    if len(split) > 0:
        values = shard_levels(key, extent, split, -0.22, 0.18) * values
    return jnp.clip(values, min=-bound, max=bound).astype(held_as)


def setup_inputs(seed: int = 0) -> dict:
    key_of = jax.random.split(jax.random.key(seed), 5)
    return {
        "fine_field": draw_fine_field(jax.random.fold_in(key_of[4], 71), 0),
        "site_map": jax.vmap(lambda own: jax.random.permutation(own, XC * YC * BLK))(jax.random.split(key_of[1], Z * T_SIZE)).reshape((Z, T_SIZE, XC * YC * BLK)).astype(jnp.int32),
        "prolongator": bell_draw(key_of[2], (Z, T_SIZE, XC * YC, NC, BLK * SPIN), 0.02, 0.119628906, ((0, 4), (1, 8))),
        "coarse_op": draw_coarse_op(jax.random.fold_in(key_of[4], 71), 0),
    }


def hop_vectors(vector):
    slabs_z, slabs_t = (vector.shape[0], vector.shape[1])
    grid = vector.reshape(slabs_z, slabs_t, XC, YC, NC, RHS)

    def flatten(values):
        return values.reshape(vector.shape)
    return [vector, flatten(jnp.roll(grid, -1, 2)), flatten(jnp.roll(grid, 1, 2)), flatten(jnp.roll(grid, -1, 3)), flatten(jnp.roll(grid, 1, 3)), jnp.roll(vector, -1, 0), jnp.roll(vector, 1, 0), jnp.roll(vector, -1, 1), jnp.roll(vector, 1, 1)]

def apply_blocks(coarse_op, vector):
    stacked = jnp.stack(hop_vectors(vector), axis=3)

    def one_slab(pair):
        return jnp.einsum('tahij,tahjr->tair', pair[0].astype(jnp.float32), pair[1].astype(jnp.float32), precision=lax.Precision.HIGHEST)
    return lax.map(one_slab, (coarse_op, stacked))

def place_rows(rows, where):
    return jnp.zeros_like(rows).at[where].set(rows)

def reference(fine_field, site_map, prolongator, coarse_op):
    slabs_z, slabs_t = (fine_field.shape[0], fine_field.shape[1])
    ordered = jnp.take_along_axis(fine_field, site_map[..., None], axis=2)
    ordered = ordered.reshape(slabs_z, slabs_t, XC * YC, BLK * SPIN, RHS)

    def restrict_slab(pair):
        return jnp.einsum('tacm,tamr->tacr', pair[0].astype(jnp.float32), pair[1].astype(jnp.float32), precision=lax.Precision.HIGHEST)
    restricted = lax.map(restrict_slab, (prolongator, ordered)).astype(jnp.bfloat16)
    first_iter = (0.5 * restricted.astype(jnp.float32)).astype(jnp.bfloat16)
    first_resid = restricted.astype(jnp.float32) - apply_blocks(coarse_op, first_iter)
    second_iter = (first_iter.astype(jnp.float32) + 0.5 * first_resid).astype(jnp.bfloat16)
    coarse_residual = restricted.astype(jnp.float32) - apply_blocks(coarse_op, second_iter)
    third_iter = (second_iter.astype(jnp.float32) + 0.5 * coarse_residual).astype(jnp.bfloat16)

    def lift_slab(pair):
        return jnp.einsum('tacm,tacr->tamr', pair[0].astype(jnp.float32), pair[1].astype(jnp.float32), precision=lax.Precision.HIGHEST)
    lifted = lax.map(lift_slab, (prolongator, third_iter)).astype(jnp.bfloat16)
    lifted = lifted.reshape(slabs_z, slabs_t, XC * YC * BLK, SPIN * RHS)
    correction = jax.vmap(jax.vmap(place_rows))(lifted, site_map)
    residual_norm = jnp.sqrt(lax.optimization_barrier(jnp.sum(coarse_residual * coarse_residual, axis=(0, 1, 2, 3))) + 1e-06)
    return (correction, coarse_residual, residual_norm)
```

```python
import functools

import jax
import jax.numpy as jnp
from jax import lax
from jax.experimental import pallas as pl
from jax.experimental.pallas import tpu as pltpu
from jax.sharding import PartitionSpec as P

SPIN = 24
XC = 4
YC = 2
SITES = XC * YC
LANES = 128
RHS = 16
STEP = 32
MESH = pl.DeviceIdType.MESH


def lane_group(shape):
    return lax.broadcasted_iota(jnp.int32, shape, len(shape) - 1) // RHS


def restrict_kernel(map_ref, fine_ref, prol_ref, rest_ref, wide):
    agg = pl.program_id(0)
    rows = fine_ref.shape[2]
    sites = rows // SITES

    @pl.when(agg == 0)
    def _():
        def widen(index, carry):
            at = pl.ds(pl.multiple_of(index * 64, 64), 64)
            for g in range(3):
                wide[g, at, :] = fine_ref[0, 0, at, g * LANES:(g + 1) * LANES].astype(jnp.float32)
            return carry
        lax.fori_loop(0, rows // 64, widen, 0)

    diagonal = lax.broadcasted_iota(jnp.int32, (8, LANES), 0) == lane_group((8, LANES))

    def body(chunk, acc):
        parts = []
        for k in range(STEP):
            row = map_ref[0, 0, agg * sites + chunk * STEP + k]
            for g in range(3):
                one = jnp.broadcast_to(wide[g, pl.ds(row, 1), :], (8, LANES))
                parts.append(jnp.where(diagonal, one, 0.0))
        tiles = [
            jnp.concatenate(parts[i:i + 2], axis=0).astype(jnp.bfloat16)
            for i in range(0, len(parts), 2)
        ]
        spread = jnp.concatenate(tiles, axis=0)
        width = STEP * SPIN
        block = prol_ref[0, 0, 0, :, pl.ds(pl.multiple_of(chunk * width, width), width)]
        return acc + jnp.dot(block, spread, preferred_element_type=jnp.float32)

    coarse = prol_ref.shape[3]
    acc = lax.fori_loop(0, sites // STEP, body, jnp.zeros((coarse, LANES), jnp.float32))
    for shift in (16, 32, 64):
        acc = acc + pltpu.roll(acc, shift, 1)
    acc = acc.astype(jnp.bfloat16).astype(jnp.float32)
    group = lane_group(acc.shape)
    rest_ref[...] = jnp.where(group == agg, acc, rest_ref[...])


def richardson_kernel(
    nz, nt, rest_ref, op_ref, resid_ref, norm_ref, third_ref,
    packed, sent, halo, part, sums_z, sums_t,
    send_sem, recv_sem, zs_sem, zr_sem, ts_sem, tr_sem,
):
    z, t = lax.axis_index("gx"), lax.axis_index("ta")
    barrier = pltpu.get_barrier_semaphore()
    for d in range(1, nz):
        pl.semaphore_signal(barrier, inc=1, device_id=(lax.rem(z + d, nz), t), device_id_type=MESH)
    for d in range(1, nt):
        pl.semaphore_signal(barrier, inc=1, device_id=(z, lax.rem(t + d, nt)), device_id_type=MESH)

    rest = rest_ref[...]
    coarse = rest.shape[0]
    first = 0.5 * rest
    sent[0] = first.astype(jnp.bfloat16)

    targets = (
        (lax.rem(z + nz - 1, nz), t),
        (lax.rem(z + 1, nz), t),
        (z, lax.rem(t + nt - 1, nt)),
        (z, lax.rem(t + 1, nt)),
    )

    def exchange(turn):
        copies = []
        for slot, target in enumerate(targets):
            copy = pltpu.make_async_remote_copy(
                src_ref=sent.at[turn],
                dst_ref=halo.at[turn, pl.ds(slot * coarse, coarse)],
                send_sem=send_sem.at[turn, slot],
                recv_sem=recv_sem.at[turn, slot],
                device_id=target,
                device_id_type=MESH,
            )
            copy.start()
            copies.append(copy)
        return copies

    group = lane_group(rest.shape)
    even = lax.rem(group, 2) == 0

    def pick(full):
        result = full[0:coarse]
        for s in range(1, SITES):
            result = jnp.where(group == s, full[s * coarse:(s + 1) * coarse], result)
        return result

    def apply_blocks(values, turn, copies):
        up = pltpu.roll(values, LANES - YC * RHS, 1)
        down = pltpu.roll(values, YC * RHS, 1)
        swap = jnp.where(even, pltpu.roll(values, LANES - RHS, 1), pltpu.roll(values, RHS, 1))
        zero = jnp.zeros_like(values)
        stack = jnp.concatenate([values, up, down, swap, swap, zero], axis=0).astype(jnp.bfloat16)
        full = jnp.dot(packed[:, 4 * coarse:], stack, preferred_element_type=jnp.float32)
        near = pick(full)
        for copy in copies:
            copy.wait()
        far = jnp.dot(packed[:, :4 * coarse], halo[turn], preferred_element_type=jnp.float32)
        return near + pick(far)

    pl.semaphore_wait(barrier, nz - 1 + nt - 1)
    copies = exchange(0)
    for h in range(9):
        at = (h - 5 if h >= 5 else h + 4) * coarse
        for s in range(SITES):
            packed[s * coarse:(s + 1) * coarse, at:at + coarse] = op_ref[0, 0, s, h]
    packed[:, 9 * coarse:] = jnp.zeros((SITES * coarse, coarse), jnp.bfloat16)
    first_resid = rest - apply_blocks(first, 0, copies)
    second_low = (first + 0.5 * first_resid).astype(jnp.bfloat16)
    sent[1] = second_low
    copies = exchange(1)
    second = second_low.astype(jnp.float32)
    resid = rest - apply_blocks(second, 1, copies)

    total = jnp.sum((resid * resid).reshape(coarse // 8, 8, LANES), axis=0)
    for shift in (16, 32, 64):
        total = total + pltpu.roll(total, shift, 1)
    part[0] = total

    def gather(turn, count, device, sums, s_sem, r_sem):
        pending = []
        for d in range(1, count):
            copy = pltpu.make_async_remote_copy(
                src_ref=part.at[turn],
                dst_ref=sums.at[d - 1],
                send_sem=s_sem.at[d - 1],
                recv_sem=r_sem.at[d - 1],
                device_id=device(d),
                device_id_type=MESH,
            )
            copy.start()
            pending.append(copy)
        return pending

    along_z = gather(0, nz, lambda d: (lax.rem(z + d, nz), t), sums_z, zs_sem, zr_sem)
    third = (second + 0.5 * resid).astype(jnp.bfloat16).astype(jnp.float32)
    third_ref[...] = jnp.transpose(third).astype(jnp.bfloat16)
    for copy in along_z:
        copy.wait()
    for d in range(nz - 1):
        total = total + sums_z[d]
    part[1] = total
    along_t = gather(1, nt, lambda d: (z, lax.rem(t + d, nt)), sums_t, ts_sem, tr_sem)
    for s in range(SITES):
        resid_ref[0, 0, s] = resid[:, s * RHS:(s + 1) * RHS]
    for copy in along_t:
        copy.wait()
    for d in range(nt - 1):
        total = total + sums_t[d]
    norm_ref[...] = jnp.sqrt(jnp.sum(total, axis=0, keepdims=True) + 1e-06)


def lift_kernel(map_ref, third_ref, prol_ref, out_ref, held, placed):
    agg = pl.program_id(0)
    rows = out_ref.shape[2]
    sites = rows // SITES
    values = third_ref[pl.ds(pl.multiple_of(agg * RHS, RHS), RHS), :]
    masks = [
        (lax.rem(lax.broadcasted_iota(jnp.int32, (RHS, 256), 1), 8) == i)
        .astype(jnp.float32).astype(jnp.bfloat16)
        for i in range(8)
    ]
    folds = (
        lax.broadcasted_iota(jnp.int32, (32, 256), 0)
        == lax.broadcasted_iota(jnp.int32, (32, 256), 1) // 8
    ).astype(jnp.float32).astype(jnp.bfloat16)
    width = STEP * SPIN

    def body(chunk, carry):
        block = prol_ref[0, 0, 0, :, pl.ds(pl.multiple_of(chunk * width, width), width)]
        flat = jnp.dot(values, block, preferred_element_type=jnp.float32).astype(jnp.bfloat16)
        base = chunk * (width // 8)
        for u in range(width // 256):
            piece = flat[:, u * 256:(u + 1) * 256]
            spread = jnp.concatenate([piece * masks[i] for i in range(8)], axis=0)
            held[pl.ds(pl.multiple_of(base + u * 32, 32), 32), :] = lax.dot_general(
                folds, spread, (((1,), (1,)), ((), ())), preferred_element_type=jnp.float32
            )
        for k in range(STEP):
            row = map_ref[0, 0, agg * sites + chunk * STEP + k]
            placed[pl.ds(pl.multiple_of(row * 8, 8), 8), :] = held[pl.ds(base + 3 * k, 8), :]
        return carry

    lax.fori_loop(0, sites // STEP, body, 0)

    @pl.when(agg == SITES - 1)
    def _():
        def narrow(index, carry):
            at = pl.ds(pl.multiple_of(index * 64, 64), 64)
            for g in range(3):
                out_ref[0, 0, at, g * LANES:(g + 1) * LANES] = placed[
                    pl.ds(index * 512 + g, 64, stride=8), :
                ].astype(jnp.bfloat16)
            return carry
        lax.fori_loop(0, rows // 64, narrow, 0)


def local(nz, nt, fine_field, site_map, prolongator, coarse_op):
    rows, columns = fine_field.shape[2:]
    coarse, depth = prolongator.shape[3:]
    whole_map = pl.BlockSpec(memory_space=pltpu.SMEM)
    vmem = pl.BlockSpec(memory_space=pltpu.VMEM)
    one_aggregate = pl.BlockSpec((1, 1, 1, coarse, depth), lambda a: (0, 0, a, 0, 0))
    whole_field = pl.BlockSpec((1, 1, rows, columns), lambda a: (0, 0, 0, 0))
    limit = 48 * 1024 * 1024

    restricted = pl.pallas_call(
        restrict_kernel,
        grid=(SITES,),
        out_shape=jax.ShapeDtypeStruct((coarse, LANES), jnp.float32),
        in_specs=[whole_map, whole_field, one_aggregate],
        out_specs=pl.BlockSpec((coarse, LANES), lambda a: (0, 0)),
        scratch_shapes=[pltpu.VMEM((3, rows, LANES), jnp.float32)],
        compiler_params=pltpu.CompilerParams(vmem_limit_bytes=limit),
    )(site_map, fine_field, prolongator)

    dma = pltpu.SemaphoreType.DMA
    coarse_residual, norm, third = pl.pallas_call(
        functools.partial(richardson_kernel, nz, nt),
        out_shape=(
            jax.ShapeDtypeStruct((1, 1, SITES, coarse, RHS), jnp.float32),
            jax.ShapeDtypeStruct((1, LANES), jnp.float32),
            jax.ShapeDtypeStruct((LANES, coarse), jnp.bfloat16),
        ),
        in_specs=[vmem, vmem],
        out_specs=(vmem, vmem, vmem),
        scratch_shapes=[
            pltpu.VMEM((SITES * coarse, 10 * coarse), jnp.bfloat16),
            pltpu.VMEM((2, coarse, LANES), jnp.bfloat16),
            pltpu.VMEM((2, 4 * coarse, LANES), jnp.bfloat16),
            pltpu.VMEM((2, 8, LANES), jnp.float32),
            pltpu.VMEM((nz - 1, 8, LANES), jnp.float32),
            pltpu.VMEM((nt - 1, 8, LANES), jnp.float32),
            dma((2, 4)),
            dma((2, 4)),
            dma((nz - 1,)),
            dma((nz - 1,)),
            dma((nt - 1,)),
            dma((nt - 1,)),
        ],
        compiler_params=pltpu.CompilerParams(
            collective_id=0, has_side_effects=True, vmem_limit_bytes=limit
        ),
    )(restricted, coarse_op)

    correction = pl.pallas_call(
        lift_kernel,
        grid=(SITES,),
        out_shape=jax.ShapeDtypeStruct(fine_field.shape, fine_field.dtype),
        in_specs=[whole_map, vmem, one_aggregate],
        out_specs=whole_field,
        scratch_shapes=[
            pltpu.VMEM((rows // SITES * 3 + 8, LANES), jnp.float32),
            pltpu.VMEM((rows * 8, LANES), jnp.float32),
        ],
        compiler_params=pltpu.CompilerParams(vmem_limit_bytes=limit),
    )(site_map, third, prolongator)
    return (correction, coarse_residual, norm[0, :RHS])


def solution(mesh):
    placed = (
        P("gx", "ta", None, None),
        P("gx", "ta", None),
        P("gx", "ta", None, None, None),
        P("gx", "ta", None, None, None, None),
    )
    return jax.shard_map(
        functools.partial(local, mesh.shape["gx"], mesh.shape["ta"]),
        mesh=mesh,
        in_specs=placed,
        out_specs=(P("gx", "ta", None, None), P("gx", "ta", None, None, None), P()),
        check_vma=False,
    )
```

```python
import functools

import jax
import jax.numpy as jnp
from jax import lax
from jax.experimental import pallas as pl
from jax.experimental.pallas import tpu as pltpu
from jax.sharding import PartitionSpec as P

SPIN = 24
XC = 4
YC = 2
SITES = XC * YC
LANES = 128
RHS = 16
STEP = 32
MESH = pl.DeviceIdType.MESH


def lane_group(shape):
    return lax.broadcasted_iota(jnp.int32, shape, len(shape) - 1) // RHS


def restrict_kernel(
    map_ref, fine_hbm, prol_hbm, rest_ref, inverse_ref, fine, prol, wide, field_sem, prol_sem
):
    rows = fine.shape[0]
    sites = rows // SITES
    coarse = prol.shape[1]
    parts = 4
    size = rows // parts

    def field_copy(n):
        at = pl.ds(n * size, size)
        return pltpu.make_async_copy(fine_hbm.at[0, 0, at], fine.at[at], field_sem.at[n])

    def prol_copy(n):
        return pltpu.make_async_copy(prol_hbm.at[0, 0, n], prol.at[n], prol_sem.at[n])

    for n in range(parts):
        field_copy(n).start()
    for n in range(SITES):
        prol_copy(n).start()
    for n in range(parts):
        field_copy(n).wait()

        def widen(index, carry):
            at = pl.ds(pl.multiple_of(n * size + index * 64, 64), 64)
            for g in range(3):
                wide[g, at, :] = fine[at, g * LANES:(g + 1) * LANES].astype(jnp.float32)
            return carry
        lax.fori_loop(0, size // 64, widen, 0)

    diagonal = lax.broadcasted_iota(jnp.int32, (8, LANES), 0) == lane_group((8, LANES))
    group = lane_group((coarse, LANES))

    def one_aggregate(agg, packed):
        prol_copy(agg).wait()

        def body(chunk, acc):
            parts = []
            for k in range(STEP):
                at = agg * sites + chunk * STEP + k
                row = map_ref[0, 0, at]
                inverse_ref[0, row] = at
                for g in range(3):
                    one = jnp.broadcast_to(wide[g, pl.ds(row, 1), :], (8, LANES))
                    parts.append(jnp.where(diagonal, one, 0.0))
            tiles = [
                jnp.concatenate(parts[i:i + 2], axis=0).astype(jnp.bfloat16)
                for i in range(0, len(parts), 2)
            ]
            spread = jnp.concatenate(tiles, axis=0)
            width = STEP * SPIN
            block = prol[agg, :, pl.ds(pl.multiple_of(chunk * width, width), width)]
            return acc + jnp.dot(block, spread, preferred_element_type=jnp.float32)

        acc = lax.fori_loop(
            0, sites // STEP, body, jnp.zeros((coarse, LANES), jnp.float32), unroll=True
        )
        for shift in (16, 32, 64):
            acc = acc + pltpu.roll(acc, shift, 1)
        acc = acc.astype(jnp.bfloat16).astype(jnp.float32)
        return jnp.where(group == agg, acc, packed)

    rest_ref[...] = lax.fori_loop(
        0, SITES, one_aggregate, jnp.zeros((coarse, LANES), jnp.float32)
    )


def richardson_kernel(
    nz, nt, inverse_ref, rest_ref, op_ref, prol_hbm, out_ref, resid_ref, norm_ref,
    prol, deal, lines, held, placed, packed, sent, halo, part, sums_z, sums_t,
    prol_sem, send_sem, recv_sem, zs_sem, zr_sem, ts_sem, tr_sem,
):
    blocks = [
        pltpu.make_async_copy(prol_hbm.at[0, 0, n], prol.at[n], prol_sem.at[n])
        for n in range(SITES)
    ]
    for copy in blocks:
        copy.start()
    z, t = lax.axis_index("gx"), lax.axis_index("ta")
    barrier = pltpu.get_barrier_semaphore()
    for d in range(1, nz):
        pl.semaphore_signal(barrier, inc=1, device_id=(lax.rem(z + d, nz), t), device_id_type=MESH)
    for d in range(1, nt):
        pl.semaphore_signal(barrier, inc=1, device_id=(z, lax.rem(t + d, nt)), device_id_type=MESH)

    rest = rest_ref[...]
    coarse = rest.shape[0]
    first = 0.5 * rest
    sent[0] = first.astype(jnp.bfloat16)

    targets = (
        (lax.rem(z + nz - 1, nz), t),
        (lax.rem(z + 1, nz), t),
        (z, lax.rem(t + nt - 1, nt)),
        (z, lax.rem(t + 1, nt)),
    )

    def exchange(turn):
        copies = []
        for slot, target in enumerate(targets):
            copy = pltpu.make_async_remote_copy(
                src_ref=sent.at[turn],
                dst_ref=halo.at[turn, pl.ds(slot * coarse, coarse)],
                send_sem=send_sem.at[turn, slot],
                recv_sem=recv_sem.at[turn, slot],
                device_id=target,
                device_id_type=MESH,
            )
            copy.start()
            copies.append(copy)
        return copies

    group = lane_group(rest.shape)
    even = lax.rem(group, 2) == 0

    def pick(full):
        result = full[0:coarse]
        for s in range(1, SITES):
            result = jnp.where(group == s, full[s * coarse:(s + 1) * coarse], result)
        return result

    depth = prol.shape[2]
    rows = out_ref.shape[2]

    line = lax.broadcasted_iota(jnp.int32, (256, 256), 0)
    column = lax.broadcasted_iota(jnp.int32, (256, 256), 1)
    for u in range(4):
        turned = lax.rem(lax.rem(column, LANES) // 32 + (4 - u), 4)
        source = 8 * lax.rem(column, 32) + 4 * (column // LANES) + turned
        deal[u] = (line == source).astype(jnp.float32).astype(jnp.bfloat16)

    def deal_lanes(begin, end):
        def body(index, carry):
            for u in range(4):
                at = pl.ds(pl.multiple_of(index * 1024 + u * 256, 256), 256)
                block = prol[:, :, at].reshape(SITES * coarse, 256)
                moved = jnp.dot(block, deal[u], preferred_element_type=jnp.float32)
                prol[:, :, at] = moved.astype(jnp.bfloat16).reshape(SITES, coarse, 256)
            return carry
        lax.fori_loop(begin, end, body, 0)

    pieces = depth // 1024

    def apply_blocks(values, turn, copies):
        up = pltpu.roll(values, LANES - YC * RHS, 1)
        down = pltpu.roll(values, YC * RHS, 1)
        swap = jnp.where(even, pltpu.roll(values, LANES - RHS, 1), pltpu.roll(values, RHS, 1))
        zero = jnp.zeros_like(values)
        stack = jnp.concatenate([values, up, down, swap, swap, zero], axis=0).astype(jnp.bfloat16)
        full = jnp.dot(packed[:, 4 * coarse:], stack, preferred_element_type=jnp.float32)
        near = pick(full)
        deal_lanes(turn * pieces // 2, (turn + 1) * pieces // 2)
        for copy in copies:
            copy.wait()
        far = jnp.dot(packed[:, :4 * coarse], halo[turn], preferred_element_type=jnp.float32)
        return near + pick(far)

    pl.semaphore_wait(barrier, nz - 1 + nt - 1)
    copies = exchange(0)
    for h in range(9):
        at = (h - 5 if h >= 5 else h + 4) * coarse
        for s in range(SITES):
            packed[s * coarse:(s + 1) * coarse, at:at + coarse] = op_ref[0, 0, s, h]
    for copy in blocks:
        copy.wait()
    packed[:, 9 * coarse:] = jnp.zeros((SITES * coarse, coarse), jnp.bfloat16)
    first_resid = rest - apply_blocks(first, 0, copies)
    second_low = (first + 0.5 * first_resid).astype(jnp.bfloat16)
    sent[1] = second_low
    copies = exchange(1)
    second = second_low.astype(jnp.float32)
    resid = rest - apply_blocks(second, 1, copies)

    total = jnp.sum((resid * resid).reshape(coarse // 8, 8, LANES), axis=0)
    for shift in (16, 32, 64):
        total = total + pltpu.roll(total, shift, 1)
    part[0] = total

    def gather(turn, count, device, sums, s_sem, r_sem):
        pending = []
        for d in range(1, count):
            copy = pltpu.make_async_remote_copy(
                src_ref=part.at[turn],
                dst_ref=sums.at[d - 1],
                send_sem=s_sem.at[d - 1],
                recv_sem=r_sem.at[d - 1],
                device_id=device(d),
                device_id_type=MESH,
            )
            copy.start()
            pending.append(copy)
        return pending

    along_z = gather(0, nz, lambda d: (lax.rem(z + d, nz), t), sums_z, zs_sem, zr_sem)
    third = (second + 0.5 * resid).astype(jnp.bfloat16).astype(jnp.float32)
    lines[...] = jnp.transpose(third).astype(jnp.bfloat16)
    spot = lax.broadcasted_iota(jnp.int32, (RHS, LANES), 1) // 32
    quarter = lax.rem(lane_group((32, LANES)), 4)

    def lift(agg):
        left = lines[pl.ds(pl.multiple_of(agg * RHS, RHS), RHS), :]
        for b in range(pieces):
            flat = jnp.dot(
                left, prol[agg, :, b * 1024:(b + 1) * 1024], preferred_element_type=jnp.float32
            )
            stacked = []
            for i in range(8):
                half = i // 4 * LANES
                piece = flat[:, half:half + LANES]
                for u in range(1, 4):
                    other = flat[:, u * 256 + half:u * 256 + half + LANES]
                    piece = jnp.where(spot == (i + u) % 4, other, piece)
                stacked.append(piece)
            turned = jnp.transpose(jnp.concatenate(stacked, axis=0))
            for u in range(4):
                piece = turned[u * 32:(u + 1) * 32]
                for i in range(1, 4):
                    from_row = (i + u) % 4 * 32
                    piece = jnp.where(quarter == i, turned[from_row:from_row + 32], piece)
                at = agg * (depth // 8) + b * LANES + u * 32
                held[pl.ds(pl.multiple_of(at, 32), 32), :] = piece

    def lift_range(begin, end):
        def body(agg, carry):
            lift(agg)
            return carry
        lax.fori_loop(begin, end, body, 0)

    lift_range(0, SITES // 2)
    for copy in along_z:
        copy.wait()
    for d in range(nz - 1):
        total = total + sums_z[d]
    part[1] = total
    along_t = gather(1, nt, lambda d: (z, lax.rem(t + d, nt)), sums_t, ts_sem, tr_sem)
    for s in range(SITES):
        resid_ref[0, 0, s] = resid[:, s * RHS:(s + 1) * RHS]
    lift_range(SITES // 2, SITES)
    held[pl.ds(3 * rows, 8), :] = jnp.zeros((8, LANES), jnp.float32)

    def place(index, carry):
        for k in range(STEP):
            at = index * STEP + k
            source = inverse_ref[0, at]
            placed[pl.ds(pl.multiple_of(at * 8, 8), 8), :] = held[pl.ds(3 * source, 8), :]
        return carry
    lax.fori_loop(0, rows // STEP, place, 0)

    def narrow(index, carry):
        at = pl.ds(pl.multiple_of(index * 64, 64), 64)
        for g in range(3):
            out_ref[0, 0, at, g * LANES:(g + 1) * LANES] = placed[
                pl.ds(index * 512 + g, 64, stride=8), :
            ].astype(jnp.bfloat16)
        return carry
    lax.fori_loop(0, rows // 64, narrow, 0)
    for copy in along_t:
        copy.wait()
    for d in range(nt - 1):
        total = total + sums_t[d]
    norm_ref[...] = jnp.sqrt(jnp.sum(total, axis=0, keepdims=True) + 1e-06)


def local(nz, nt, fine_field, site_map, prolongator, coarse_op):
    rows, columns = fine_field.shape[2:]
    coarse, depth = prolongator.shape[3:]
    smem = pl.BlockSpec(memory_space=pltpu.SMEM)
    vmem = pl.BlockSpec(memory_space=pltpu.VMEM)
    hbm = pl.BlockSpec(memory_space=pl.ANY)
    dma = pltpu.SemaphoreType.DMA
    limit = 58 * 1024 * 1024

    restricted, inverse = pl.pallas_call(
        restrict_kernel,
        out_shape=(
            jax.ShapeDtypeStruct((coarse, LANES), jnp.float32),
            jax.ShapeDtypeStruct((1, rows), jnp.int32),
        ),
        in_specs=[smem, hbm, hbm],
        out_specs=(vmem, smem),
        scratch_shapes=[
            pltpu.VMEM((rows, columns), jnp.bfloat16),
            pltpu.VMEM((SITES, coarse, depth), jnp.bfloat16),
            pltpu.VMEM((3, rows, LANES), jnp.float32),
            dma((4,)),
            dma((SITES,)),
        ],
        compiler_params=pltpu.CompilerParams(vmem_limit_bytes=limit),
    )(site_map, fine_field, prolongator)

    correction, coarse_residual, norm = pl.pallas_call(
        functools.partial(richardson_kernel, nz, nt),
        out_shape=(
            jax.ShapeDtypeStruct(fine_field.shape, fine_field.dtype),
            jax.ShapeDtypeStruct((1, 1, SITES, coarse, RHS), jnp.float32),
            jax.ShapeDtypeStruct((1, LANES), jnp.float32),
        ),
        in_specs=[smem, vmem, vmem, hbm],
        out_specs=(vmem, vmem, vmem),
        scratch_shapes=[
            pltpu.VMEM((SITES, coarse, depth), jnp.bfloat16),
            pltpu.VMEM((4, 256, 256), jnp.bfloat16),
            pltpu.VMEM((LANES, coarse), jnp.bfloat16),
            pltpu.VMEM((rows * 3 + 8, LANES), jnp.float32),
            pltpu.VMEM((rows * 8, LANES), jnp.float32),
            pltpu.VMEM((SITES * coarse, 10 * coarse), jnp.bfloat16),
            pltpu.VMEM((2, coarse, LANES), jnp.bfloat16),
            pltpu.VMEM((2, 4 * coarse, LANES), jnp.bfloat16),
            pltpu.VMEM((2, 8, LANES), jnp.float32),
            pltpu.VMEM((nz - 1, 8, LANES), jnp.float32),
            pltpu.VMEM((nt - 1, 8, LANES), jnp.float32),
            dma((SITES,)),
            dma((2, 4)),
            dma((2, 4)),
            dma((nz - 1,)),
            dma((nz - 1,)),
            dma((nt - 1,)),
            dma((nt - 1,)),
        ],
        compiler_params=pltpu.CompilerParams(
            collective_id=0, has_side_effects=True, vmem_limit_bytes=limit
        ),
    )(inverse, restricted, coarse_op, prolongator)
    return (correction, coarse_residual, norm[0, :RHS])


def solution(mesh):
    placed = (
        P("gx", "ta", None, None),
        P("gx", "ta", None),
        P("gx", "ta", None, None, None),
        P("gx", "ta", None, None, None, None),
    )
    return jax.shard_map(
        functools.partial(local, mesh.shape["gx"], mesh.shape["ta"]),
        mesh=mesh,
        in_specs=placed,
        out_specs=(P("gx", "ta", None, None), P("gx", "ta", None, None, None), P()),
        check_vma=False,
    )
```

```python
import functools

import jax
import jax.numpy as jnp
from jax import lax
from jax.experimental import pallas as pl
from jax.experimental.pallas import tpu as pltpu
from jax.sharding import PartitionSpec as P

SPIN = 24
XC = 4
YC = 2
SITES = XC * YC
LANES = 128
RHS = 16
STEP = 32
MESH = pl.DeviceIdType.MESH


def lane_group(shape):
    return lax.broadcasted_iota(jnp.int32, shape, len(shape) - 1) // RHS


def restrict_kernel(
    map_ref, fine_hbm, prol_hbm, rest_ref, prol, fine, wide, field_sem, prol_sem
):
    rows = fine.shape[0]
    sites = rows // SITES
    coarse = prol.shape[1]
    parts = 4
    size = rows // parts

    def field_copy(n):
        at = pl.ds(n * size, size)
        return pltpu.make_async_copy(fine_hbm.at[0, 0, at], fine.at[at], field_sem.at[n])

    def prol_copy(n):
        return pltpu.make_async_copy(prol_hbm.at[0, 0, n], prol.at[n], prol_sem.at[n])

    for n in range(parts):
        field_copy(n).start()
    for n in range(SITES):
        prol_copy(n).start()
    for n in range(parts):
        field_copy(n).wait()

        def widen(index, carry):
            at = pl.ds(pl.multiple_of(n * size + index * 64, 64), 64)
            for g in range(3):
                wide[g, at, :] = fine[at, g * LANES:(g + 1) * LANES].astype(jnp.float32)
            return carry
        lax.fori_loop(0, size // 64, widen, 0)

    diagonal = lax.broadcasted_iota(jnp.int32, (8, LANES), 0) == lane_group((8, LANES))
    group = lane_group((coarse, LANES))

    def one_aggregate(agg, packed):
        prol_copy(agg).wait()

        def body(chunk, acc):
            parts = []
            for k in range(STEP):
                row = map_ref[0, 0, agg * sites + chunk * STEP + k]
                for g in range(3):
                    one = jnp.broadcast_to(wide[g, pl.ds(row, 1), :], (8, LANES))
                    parts.append(jnp.where(diagonal, one, 0.0))
            tiles = [
                jnp.concatenate(parts[i:i + 2], axis=0).astype(jnp.bfloat16)
                for i in range(0, len(parts), 2)
            ]
            spread = jnp.concatenate(tiles, axis=0)
            width = STEP * SPIN
            block = prol[agg, :, pl.ds(pl.multiple_of(chunk * width, width), width)]
            return acc + jnp.dot(block, spread, preferred_element_type=jnp.float32)

        acc = lax.fori_loop(
            0, sites // STEP, body, jnp.zeros((coarse, LANES), jnp.float32), unroll=True
        )
        for shift in (16, 32, 64):
            acc = acc + pltpu.roll(acc, shift, 1)
        acc = acc.astype(jnp.bfloat16).astype(jnp.float32)
        return jnp.where(group == agg, acc, packed)

    rest_ref[...] = lax.fori_loop(
        0, SITES, one_aggregate, jnp.zeros((coarse, LANES), jnp.float32)
    )


def richardson_kernel(
    nz, nt, rest_ref, op_ref, source, held, resid_ref, norm_ref,
    prol, deal, lines, packed, sent, halo, part, sums_z, sums_t,
    send_sem, recv_sem, zs_sem, zr_sem, ts_sem, tr_sem,
):
    z, t = lax.axis_index("gx"), lax.axis_index("ta")
    barrier = pltpu.get_barrier_semaphore()
    for d in range(1, nz):
        pl.semaphore_signal(barrier, inc=1, device_id=(lax.rem(z + d, nz), t), device_id_type=MESH)
    for d in range(1, nt):
        pl.semaphore_signal(barrier, inc=1, device_id=(z, lax.rem(t + d, nt)), device_id_type=MESH)

    rest = rest_ref[...]
    coarse = rest.shape[0]
    first = 0.5 * rest
    sent[0] = first.astype(jnp.bfloat16)

    targets = (
        (lax.rem(z + nz - 1, nz), t),
        (lax.rem(z + 1, nz), t),
        (z, lax.rem(t + nt - 1, nt)),
        (z, lax.rem(t + 1, nt)),
    )

    def exchange(turn):
        copies = []
        for slot, target in enumerate(targets):
            copy = pltpu.make_async_remote_copy(
                src_ref=sent.at[turn],
                dst_ref=halo.at[turn, pl.ds(slot * coarse, coarse)],
                send_sem=send_sem.at[turn, slot],
                recv_sem=recv_sem.at[turn, slot],
                device_id=target,
                device_id_type=MESH,
            )
            copy.start()
            copies.append(copy)
        return copies

    group = lane_group(rest.shape)
    even = lax.rem(group, 2) == 0

    def pick(full):
        result = full[0:coarse]
        for s in range(1, SITES):
            result = jnp.where(group == s, full[s * coarse:(s + 1) * coarse], result)
        return result

    depth = prol.shape[2]

    line = lax.broadcasted_iota(jnp.int32, (256, 256), 0)
    column = lax.broadcasted_iota(jnp.int32, (256, 256), 1)
    for u in range(4):
        turned = lax.rem(lax.rem(column, LANES) // 32 + (4 - u), 4)
        origin = 8 * lax.rem(column, 32) + 4 * (column // LANES) + turned
        deal[u] = (line == origin).astype(jnp.float32).astype(jnp.bfloat16)

    def deal_lanes(begin, end):
        def body(index, carry):
            for u in range(4):
                at = pl.ds(pl.multiple_of(index * 1024 + u * 256, 256), 256)
                block = source[:, :, at].reshape(SITES * coarse, 256)
                moved = jnp.dot(block, deal[u], preferred_element_type=jnp.float32)
                prol[:, :, at] = moved.astype(jnp.bfloat16).reshape(SITES, coarse, 256)
            return carry
        lax.fori_loop(begin, end, body, 0)

    pieces = depth // 1024

    def apply_blocks(values, turn, copies):
        up = pltpu.roll(values, LANES - YC * RHS, 1)
        down = pltpu.roll(values, YC * RHS, 1)
        swap = jnp.where(even, pltpu.roll(values, LANES - RHS, 1), pltpu.roll(values, RHS, 1))
        zero = jnp.zeros_like(values)
        stack = jnp.concatenate([values, up, down, swap, swap, zero], axis=0).astype(jnp.bfloat16)
        full = jnp.dot(packed[:, 4 * coarse:], stack, preferred_element_type=jnp.float32)
        near = pick(full)
        deal_lanes(turn * pieces // 2, (turn + 1) * pieces // 2)
        for copy in copies:
            copy.wait()
        far = jnp.dot(packed[:, :4 * coarse], halo[turn], preferred_element_type=jnp.float32)
        return near + pick(far)

    pl.semaphore_wait(barrier, nz - 1 + nt - 1)
    copies = exchange(0)
    for h in range(9):
        at = (h - 5 if h >= 5 else h + 4) * coarse
        for s in range(SITES):
            packed[s * coarse:(s + 1) * coarse, at:at + coarse] = op_ref[0, 0, s, h]
    packed[:, 9 * coarse:] = jnp.zeros((SITES * coarse, coarse), jnp.bfloat16)
    first_resid = rest - apply_blocks(first, 0, copies)
    second_low = (first + 0.5 * first_resid).astype(jnp.bfloat16)
    sent[1] = second_low
    copies = exchange(1)
    second = second_low.astype(jnp.float32)
    resid = rest - apply_blocks(second, 1, copies)

    total = jnp.sum((resid * resid).reshape(coarse // 8, 8, LANES), axis=0)
    for shift in (16, 32, 64):
        total = total + pltpu.roll(total, shift, 1)
    part[0] = total

    def gather(turn, count, device, sums, s_sem, r_sem):
        pending = []
        for d in range(1, count):
            copy = pltpu.make_async_remote_copy(
                src_ref=part.at[turn],
                dst_ref=sums.at[d - 1],
                send_sem=s_sem.at[d - 1],
                recv_sem=r_sem.at[d - 1],
                device_id=device(d),
                device_id_type=MESH,
            )
            copy.start()
            pending.append(copy)
        return pending

    along_z = gather(0, nz, lambda d: (lax.rem(z + d, nz), t), sums_z, zs_sem, zr_sem)
    third = (second + 0.5 * resid).astype(jnp.bfloat16).astype(jnp.float32)
    lines[...] = jnp.transpose(third).astype(jnp.bfloat16)
    spot = lax.broadcasted_iota(jnp.int32, (RHS, LANES), 1) // 32
    quarter = lax.rem(lane_group((32, LANES)), 4)

    def lift(agg):
        left = lines[pl.ds(pl.multiple_of(agg * RHS, RHS), RHS), :]
        for b in range(pieces):
            flat = jnp.dot(
                left, prol[agg, :, b * 1024:(b + 1) * 1024], preferred_element_type=jnp.float32
            )
            stacked = []
            for i in range(8):
                half = i // 4 * LANES
                piece = flat[:, half:half + LANES]
                for u in range(1, 4):
                    other = flat[:, u * 256 + half:u * 256 + half + LANES]
                    piece = jnp.where(spot == (i + u) % 4, other, piece)
                stacked.append(piece)
            turned = jnp.transpose(jnp.concatenate(stacked, axis=0))
            for u in range(4):
                piece = turned[u * 32:(u + 1) * 32]
                for i in range(1, 4):
                    from_row = (i + u) % 4 * 32
                    piece = jnp.where(quarter == i, turned[from_row:from_row + 32], piece)
                at = agg * (depth // 8) + b * LANES + u * 32
                held[pl.ds(pl.multiple_of(at, 32), 32), :] = piece

    def lift_range(begin, end):
        def body(agg, carry):
            lift(agg)
            return carry
        lax.fori_loop(begin, end, body, 0)

    held[pl.ds(SITES * depth // 8, 8), :] = jnp.zeros((8, LANES), jnp.float32)
    lift_range(0, SITES // 2)
    for copy in along_z:
        copy.wait()
    for d in range(nz - 1):
        total = total + sums_z[d]
    part[1] = total
    along_t = gather(1, nt, lambda d: (z, lax.rem(t + d, nt)), sums_t, ts_sem, tr_sem)
    lift_range(SITES // 2, SITES)
    resid_ref[...] = jnp.transpose(resid)
    for copy in along_t:
        copy.wait()
    for d in range(nt - 1):
        total = total + sums_t[d]
    norm_ref[...] = jnp.sqrt(jnp.sum(total, axis=0, keepdims=True) + 1e-06)


def place_kernel(
    map_ref, held, resid, norm, out_hbm, resid_ref, norm_ref, placed, out, out_sem
):
    rows = out.shape[0]
    norm_ref[...] = norm[:, :RHS]
    resid_ref[0, 0] = resid[...].reshape(resid_ref.shape[2:])

    def place(index, carry):
        for k in range(STEP):
            at = index * STEP + k
            row = map_ref[0, 0, at]
            placed[pl.ds(pl.multiple_of(row * 8, 8), 8), :] = held[pl.ds(3 * at, 8), :]
        return carry
    lax.fori_loop(0, rows // STEP, place, 0)

    def copy_out(n):
        at = pl.ds(pl.multiple_of(n * 256, 256), 256)
        return pltpu.make_async_copy(out.at[at], out_hbm.at[0, 0, at], out_sem.at[n])

    def narrow(index, carry):
        for g in range(3):
            out[pl.ds(pl.multiple_of(index * 256, 256), 256), g * LANES:(g + 1) * LANES] = (
                placed[pl.ds(index * 2048 + g, 256, stride=8), :].astype(jnp.bfloat16)
            )
        copy_out(index).start()
        return carry
    lax.fori_loop(0, rows // 256, narrow, 0)

    def finish(index, carry):
        copy_out(index).wait()
        return carry
    lax.fori_loop(0, rows // 256, finish, 0)


def local(nz, nt, fine_field, site_map, prolongator, coarse_op):
    rows, columns = fine_field.shape[2:]
    coarse, depth = prolongator.shape[3:]
    smem = pl.BlockSpec(memory_space=pltpu.SMEM)
    vmem = pl.BlockSpec(memory_space=pltpu.VMEM)
    hbm = pl.BlockSpec(memory_space=pltpu.HBM)
    dma = pltpu.SemaphoreType.DMA
    limit = 36 * 1024 * 1024

    restricted, held_prolongator = pl.pallas_call(
        restrict_kernel,
        out_shape=(
            pltpu.VMEM((coarse, LANES), jnp.float32),
            pltpu.VMEM((SITES, coarse, depth), jnp.bfloat16),
        ),
        in_specs=[smem, hbm, hbm],
        out_specs=(vmem, vmem),
        scratch_shapes=[
            pltpu.VMEM((rows, columns), jnp.bfloat16),
            pltpu.VMEM((3, rows, LANES), jnp.float32),
            dma((4,)),
            dma((SITES,)),
        ],
        compiler_params=pltpu.CompilerParams(vmem_limit_bytes=57 * 1024 * 1024),
    )(site_map, fine_field, prolongator)

    held, packed_residual, norm = pl.pallas_call(
        functools.partial(richardson_kernel, nz, nt),
        out_shape=(
            pltpu.VMEM((rows * 3 + 8, LANES), jnp.float32),
            pltpu.VMEM((LANES, coarse), jnp.float32),
            pltpu.VMEM((1, LANES), jnp.float32),
        ),
        in_specs=[vmem, vmem, vmem],
        out_specs=(vmem, vmem, vmem),
        scratch_shapes=[
            pltpu.VMEM((SITES, coarse, depth), jnp.bfloat16),
            pltpu.VMEM((4, 256, 256), jnp.bfloat16),
            pltpu.VMEM((LANES, coarse), jnp.bfloat16),
            pltpu.VMEM((SITES * coarse, 10 * coarse), jnp.bfloat16),
            pltpu.VMEM((2, coarse, LANES), jnp.bfloat16),
            pltpu.VMEM((2, 4 * coarse, LANES), jnp.bfloat16),
            pltpu.VMEM((2, 8, LANES), jnp.float32),
            pltpu.VMEM((nz - 1, 8, LANES), jnp.float32),
            pltpu.VMEM((nt - 1, 8, LANES), jnp.float32),
            dma((2, 4)),
            dma((2, 4)),
            dma((nz - 1,)),
            dma((nz - 1,)),
            dma((nt - 1,)),
            dma((nt - 1,)),
        ],
        compiler_params=pltpu.CompilerParams(
            collective_id=0, has_side_effects=True, vmem_limit_bytes=limit
        ),
    )(restricted, coarse_op, held_prolongator)

    correction, coarse_residual, norm = pl.pallas_call(
        place_kernel,
        out_shape=(
            jax.ShapeDtypeStruct(fine_field.shape, fine_field.dtype),
            jax.ShapeDtypeStruct((1, 1, SITES, RHS, coarse), jnp.float32),
            jax.ShapeDtypeStruct((1, RHS), jnp.float32),
        ),
        in_specs=[smem, vmem, vmem, vmem],
        out_specs=(hbm, vmem, vmem),
        scratch_shapes=[
            pltpu.VMEM((rows * 8, LANES), jnp.float32),
            pltpu.VMEM((rows, columns), jnp.bfloat16),
            dma((rows // 256,)),
        ],
        compiler_params=pltpu.CompilerParams(vmem_limit_bytes=limit),
    )(site_map, held, packed_residual, norm)
    return (correction, jnp.swapaxes(coarse_residual, 3, 4), norm.reshape(RHS))


def solution(mesh):
    placed = (
        P("gx", "ta", None, None),
        P("gx", "ta", None),
        P("gx", "ta", None, None, None),
        P("gx", "ta", None, None, None, None),
    )
    return jax.shard_map(
        functools.partial(local, mesh.shape["gx"], mesh.shape["ta"]),
        mesh=mesh,
        in_specs=placed,
        out_specs=(P("gx", "ta", None, None), P("gx", "ta", None, None, None), P()),
        check_vma=False,
    )
```

```python
import functools

import jax
import jax.numpy as jnp
from jax import lax
from jax.experimental import pallas as pl
from jax.experimental.pallas import tpu as pltpu
from jax.sharding import PartitionSpec as P

SPIN = 24
XC = 4
YC = 2
SITES = XC * YC
LANES = 128
RHS = 16
STEP = 32
MESH = pl.DeviceIdType.MESH


def lane_group(shape):
    return lax.broadcasted_iota(jnp.int32, shape, len(shape) - 1) // RHS


def restrict_kernel(
    map_ref, fine_hbm, prol_hbm, op_hbm, rest_ref, prol, op, fine, wide, sums,
    field_sem, prol_sem, op_sem
):
    rows = fine.shape[0]
    sites = rows // SITES
    coarse = prol.shape[1]
    parts = 4
    size = rows // parts

    def field_copy(n):
        at = pl.ds(n * size, size)
        return pltpu.make_async_copy(fine_hbm.at[0, 0, at], fine.at[at], field_sem.at[n])

    def prol_copy(n):
        return pltpu.make_async_copy(prol_hbm.at[0, 0, n], prol.at[n], prol_sem.at[n])

    for n in range(parts):
        field_copy(n).start()
    for n in range(SITES):
        prol_copy(n).start()
    op_copy = pltpu.make_async_copy(op_hbm, op, op_sem)
    op_copy.start()
    for n in range(parts):
        field_copy(n).wait()

        def widen(index, carry):
            at = pl.ds(pl.multiple_of(n * size + index * 64, 64), 64)
            for g in range(3):
                wide[g, at, :] = fine[at, g * LANES:(g + 1) * LANES].astype(jnp.float32)
            return carry
        lax.fori_loop(0, size // 64, widen, 0)

    diagonal = lax.broadcasted_iota(jnp.int32, (8, LANES), 0) == lane_group((8, LANES))
    group = lane_group((coarse, LANES))

    def one_aggregate(agg, carry):
        prol_copy(agg).wait()

        def body(chunk, acc):
            parts = []
            for k in range(STEP):
                row = map_ref[0, 0, agg * sites + chunk * STEP + k]
                for g in range(3):
                    one = jnp.broadcast_to(wide[g, pl.ds(row, 1), :], (8, LANES))
                    parts.append(jnp.where(diagonal, one, 0.0))
            tiles = [
                jnp.concatenate(parts[i:i + 2], axis=0).astype(jnp.bfloat16)
                for i in range(0, len(parts), 2)
            ]
            spread = jnp.concatenate(tiles, axis=0)
            width = STEP * SPIN
            block = prol[agg, :, pl.ds(pl.multiple_of(chunk * width, width), width)]
            return acc + jnp.dot(block, spread, preferred_element_type=jnp.float32)

        sums[agg] = lax.fori_loop(
            0, sites // STEP, body, jnp.zeros((coarse, LANES), jnp.float32), unroll=True
        )
        return carry

    lax.fori_loop(0, SITES, one_aggregate, 0)
    packed = jnp.zeros((coarse, LANES), jnp.float32)
    for agg in range(SITES):
        acc = sums[agg]
        for shift in (16, 32, 64):
            acc = acc + pltpu.roll(acc, shift, 1)
        packed = jnp.where(group == agg, acc, packed)
    rest_ref[...] = packed.astype(jnp.bfloat16).astype(jnp.float32)
    op_copy.wait()


def richardson_kernel(
    nz, nt, rest_ref, op_ref, source, held, resid_ref, norm_ref,
    prol, deal, lines, packed, sent, halo, part, sums_z, sums_t,
    send_sem, recv_sem, zs_sem, zr_sem, ts_sem, tr_sem,
):
    z, t = lax.axis_index("gx"), lax.axis_index("ta")
    barrier = pltpu.get_barrier_semaphore()
    for d in range(1, nz):
        pl.semaphore_signal(barrier, inc=1, device_id=(lax.rem(z + d, nz), t), device_id_type=MESH)
    for d in range(1, nt):
        pl.semaphore_signal(barrier, inc=1, device_id=(z, lax.rem(t + d, nt)), device_id_type=MESH)

    rest = rest_ref[...]
    coarse = rest.shape[0]
    first = 0.5 * rest
    sent[0] = first.astype(jnp.bfloat16)

    targets = (
        (lax.rem(z + nz - 1, nz), t),
        (lax.rem(z + 1, nz), t),
        (z, lax.rem(t + nt - 1, nt)),
        (z, lax.rem(t + 1, nt)),
    )

    def exchange(turn):
        copies = []
        for slot, target in enumerate(targets):
            copy = pltpu.make_async_remote_copy(
                src_ref=sent.at[turn],
                dst_ref=halo.at[turn, pl.ds(slot * coarse, coarse)],
                send_sem=send_sem.at[turn, slot],
                recv_sem=recv_sem.at[turn, slot],
                device_id=target,
                device_id_type=MESH,
            )
            copy.start()
            copies.append(copy)
        return copies

    group = lane_group(rest.shape)
    even = lax.rem(group, 2) == 0

    def pick(full):
        result = full[0:coarse]
        for s in range(1, SITES):
            result = jnp.where(group == s, full[s * coarse:(s + 1) * coarse], result)
        return result

    depth = prol.shape[2]

    line = lax.broadcasted_iota(jnp.int32, (256, 256), 0)
    column = lax.broadcasted_iota(jnp.int32, (256, 256), 1)
    for u in range(4):
        turned = lax.rem(lax.rem(column, LANES) // 32 + (4 - u), 4)
        origin = 8 * lax.rem(column, 32) + 4 * (column // LANES) + turned
        deal[u] = (line == origin).astype(jnp.float32).astype(jnp.bfloat16)

    def deal_lanes(begin, end):
        def body(index, carry):
            for u in range(4):
                at = pl.ds(pl.multiple_of(index * 1024 + u * 256, 256), 256)
                block = source[:, :, at].reshape(SITES * coarse, 256)
                moved = jnp.dot(block, deal[u], preferred_element_type=jnp.float32)
                prol[:, :, at] = moved.astype(jnp.bfloat16).reshape(SITES, coarse, 256)
            return carry
        lax.fori_loop(begin, end, body, 0)

    pieces = depth // 1024

    def apply_blocks(values, turn, copies):
        up = pltpu.roll(values, LANES - YC * RHS, 1)
        down = pltpu.roll(values, YC * RHS, 1)
        swap = jnp.where(even, pltpu.roll(values, LANES - RHS, 1), pltpu.roll(values, RHS, 1))
        zero = jnp.zeros_like(values)
        stack = jnp.concatenate([values, up, down, swap, swap, zero], axis=0).astype(jnp.bfloat16)
        full = jnp.dot(packed[:, 4 * coarse:], stack, preferred_element_type=jnp.float32)
        near = pick(full)
        deal_lanes(turn * pieces // 2, (turn + 1) * pieces // 2)
        for copy in copies:
            copy.wait()
        far = jnp.dot(packed[:, :4 * coarse], halo[turn], preferred_element_type=jnp.float32)
        return near + pick(far)

    for h in range(9):
        at = (h - 5 if h >= 5 else h + 4) * coarse
        for s in range(SITES):
            packed[s * coarse:(s + 1) * coarse, at:at + coarse] = op_ref[0, 0, s, h]
    packed[:, 9 * coarse:] = jnp.zeros((SITES * coarse, coarse), jnp.bfloat16)
    pl.semaphore_wait(barrier, nz - 1 + nt - 1)
    copies = exchange(0)
    first_resid = rest - apply_blocks(first, 0, copies)
    second_low = (first + 0.5 * first_resid).astype(jnp.bfloat16)
    sent[1] = second_low
    copies = exchange(1)
    second = second_low.astype(jnp.float32)
    resid = rest - apply_blocks(second, 1, copies)

    total = jnp.sum((resid * resid).reshape(coarse // 8, 8, LANES), axis=0)
    for shift in (16, 32, 64):
        total = total + pltpu.roll(total, shift, 1)
    part[0] = total

    def gather(turn, count, device, sums, s_sem, r_sem):
        pending = []
        for d in range(1, count):
            copy = pltpu.make_async_remote_copy(
                src_ref=part.at[turn],
                dst_ref=sums.at[d - 1],
                send_sem=s_sem.at[d - 1],
                recv_sem=r_sem.at[d - 1],
                device_id=device(d),
                device_id_type=MESH,
            )
            copy.start()
            pending.append(copy)
        return pending

    along_z = gather(0, nz, lambda d: (lax.rem(z + d, nz), t), sums_z, zs_sem, zr_sem)
    third = (second + 0.5 * resid).astype(jnp.bfloat16).astype(jnp.float32)
    lines[...] = jnp.transpose(third).astype(jnp.bfloat16)
    spot = lax.broadcasted_iota(jnp.int32, (RHS, LANES), 1) // 32
    quarter = lax.rem(lane_group((32, LANES)), 4)

    def lift(agg):
        left = lines[pl.ds(pl.multiple_of(agg * RHS, RHS), RHS), :]
        for b in range(pieces):
            flat = jnp.dot(
                left, prol[agg, :, b * 1024:(b + 1) * 1024], preferred_element_type=jnp.float32
            )
            stacked = []
            for i in range(8):
                half = i // 4 * LANES
                piece = flat[:, half:half + LANES]
                for u in range(1, 4):
                    other = flat[:, u * 256 + half:u * 256 + half + LANES]
                    piece = jnp.where(spot == (i + u) % 4, other, piece)
                stacked.append(piece)
            turned = jnp.transpose(jnp.concatenate(stacked, axis=0))
            for u in range(4):
                piece = turned[u * 32:(u + 1) * 32]
                for i in range(1, 4):
                    from_row = (i + u) % 4 * 32
                    piece = jnp.where(quarter == i, turned[from_row:from_row + 32], piece)
                at = agg * (depth // 8) + b * LANES + u * 32
                held[pl.ds(pl.multiple_of(at, 32), 32), :] = piece

    def lift_range(begin, end):
        def body(agg, carry):
            lift(agg)
            return carry
        lax.fori_loop(begin, end, body, 0, unroll=2)

    held[pl.ds(SITES * depth // 8, 8), :] = jnp.zeros((8, LANES), jnp.float32)
    lift_range(0, SITES // 2)
    for copy in along_z:
        copy.wait()
    for d in range(nz - 1):
        total = total + sums_z[d]
    part[1] = total
    along_t = gather(1, nt, lambda d: (z, lax.rem(t + d, nt)), sums_t, ts_sem, tr_sem)
    lift_range(SITES // 2, SITES)
    resid_ref[...] = jnp.transpose(resid)
    for copy in along_t:
        copy.wait()
    for d in range(nt - 1):
        total = total + sums_t[d]
    norm_ref[...] = jnp.sqrt(jnp.sum(total, axis=0, keepdims=True) + 1e-06)


def place_kernel(
    map_ref, held, resid, norm, out_hbm, resid_ref, norm_ref, placed, out, out_sem
):
    rows = out.shape[0]
    norm_ref[...] = norm[:, :RHS]
    resid_ref[0, 0] = resid[...].reshape(resid_ref.shape[2:])

    def place(index, carry):
        for k in range(STEP):
            at = index * STEP + k
            row = map_ref[0, 0, at]
            placed[pl.ds(pl.multiple_of(row * 8, 8), 8), :] = held[pl.ds(3 * at, 8), :]
        return carry
    lax.fori_loop(0, rows // STEP, place, 0)

    def copy_out(n):
        at = pl.ds(pl.multiple_of(n * 256, 256), 256)
        return pltpu.make_async_copy(out.at[at], out_hbm.at[0, 0, at], out_sem.at[n])

    def narrow(index, carry):
        for g in range(3):
            out[pl.ds(pl.multiple_of(index * 256, 256), 256), g * LANES:(g + 1) * LANES] = (
                placed[pl.ds(index * 2048 + g, 256, stride=8), :].astype(jnp.bfloat16)
            )
        copy_out(index).start()
        return carry
    lax.fori_loop(0, rows // 256, narrow, 0)

    def finish(index, carry):
        copy_out(index).wait()
        return carry
    lax.fori_loop(0, rows // 256, finish, 0)


def local(nz, nt, fine_field, site_map, prolongator, coarse_op):
    rows, columns = fine_field.shape[2:]
    coarse, depth = prolongator.shape[3:]
    smem = pl.BlockSpec(memory_space=pltpu.SMEM)
    vmem = pl.BlockSpec(memory_space=pltpu.VMEM)
    hbm = pl.BlockSpec(memory_space=pltpu.HBM)
    dma = pltpu.SemaphoreType.DMA
    limit = 36 * 1024 * 1024

    restricted, held_prolongator, held_op = pl.pallas_call(
        restrict_kernel,
        out_shape=(
            pltpu.VMEM((coarse, LANES), jnp.float32),
            pltpu.VMEM((SITES, coarse, depth), jnp.bfloat16),
            pltpu.VMEM(coarse_op.shape, jnp.bfloat16),
        ),
        in_specs=[smem, hbm, hbm, hbm],
        out_specs=(vmem, vmem, vmem),
        scratch_shapes=[
            pltpu.VMEM((rows, columns), jnp.bfloat16),
            pltpu.VMEM((3, rows, LANES), jnp.float32),
            pltpu.VMEM((SITES, coarse, LANES), jnp.float32),
            dma((4,)),
            dma((SITES,)),
            dma(()),
        ],
        compiler_params=pltpu.CompilerParams(vmem_limit_bytes=56 * 1024 * 1024),
    )(site_map, fine_field, prolongator, coarse_op)

    held, packed_residual, norm = pl.pallas_call(
        functools.partial(richardson_kernel, nz, nt),
        out_shape=(
            pltpu.VMEM((rows * 3 + 8, LANES), jnp.float32),
            pltpu.VMEM((LANES, coarse), jnp.float32),
            pltpu.VMEM((1, LANES), jnp.float32),
        ),
        in_specs=[vmem, vmem, vmem],
        out_specs=(vmem, vmem, vmem),
        scratch_shapes=[
            pltpu.VMEM((SITES, coarse, depth), jnp.bfloat16),
            pltpu.VMEM((4, 256, 256), jnp.bfloat16),
            pltpu.VMEM((LANES, coarse), jnp.bfloat16),
            pltpu.VMEM((SITES * coarse, 10 * coarse), jnp.bfloat16),
            pltpu.VMEM((2, coarse, LANES), jnp.bfloat16),
            pltpu.VMEM((2, 4 * coarse, LANES), jnp.bfloat16),
            pltpu.VMEM((2, 8, LANES), jnp.float32),
            pltpu.VMEM((nz - 1, 8, LANES), jnp.float32),
            pltpu.VMEM((nt - 1, 8, LANES), jnp.float32),
            dma((2, 4)),
            dma((2, 4)),
            dma((nz - 1,)),
            dma((nz - 1,)),
            dma((nt - 1,)),
            dma((nt - 1,)),
        ],
        compiler_params=pltpu.CompilerParams(
            collective_id=0, has_side_effects=True, vmem_limit_bytes=limit
        ),
    )(restricted, held_op, held_prolongator)

    correction, coarse_residual, norm = pl.pallas_call(
        place_kernel,
        out_shape=(
            jax.ShapeDtypeStruct(fine_field.shape, fine_field.dtype),
            jax.ShapeDtypeStruct((1, 1, SITES, RHS, coarse), jnp.float32),
            jax.ShapeDtypeStruct((1, RHS), jnp.float32),
        ),
        in_specs=[smem, vmem, vmem, vmem],
        out_specs=(hbm, vmem, vmem),
        scratch_shapes=[
            pltpu.VMEM((rows * 8, LANES), jnp.float32),
            pltpu.VMEM((rows, columns), jnp.bfloat16),
            dma((rows // 256,)),
        ],
        compiler_params=pltpu.CompilerParams(vmem_limit_bytes=limit),
    )(site_map, held, packed_residual, norm)
    return (correction, jnp.swapaxes(coarse_residual, 3, 4), norm.reshape(RHS))


def solution(mesh):
    placed = (
        P("gx", "ta", None, None),
        P("gx", "ta", None),
        P("gx", "ta", None, None, None),
        P("gx", "ta", None, None, None, None),
    )
    return jax.shard_map(
        functools.partial(local, mesh.shape["gx"], mesh.shape["ta"]),
        mesh=mesh,
        in_specs=placed,
        out_specs=(P("gx", "ta", None, None), P("gx", "ta", None, None, None), P()),
        check_vma=False,
    )
```

```python
import functools

import jax
import jax.numpy as jnp
from jax import lax
from jax.experimental import pallas as pl
from jax.experimental.pallas import tpu as pltpu
from jax.sharding import PartitionSpec as P

SPIN = 24
XC = 4
YC = 2
SITES = XC * YC
LANES = 128
RHS = 16
STEP = 32
MESH = pl.DeviceIdType.MESH


def lane_group(shape):
    return lax.broadcasted_iota(jnp.int32, shape, len(shape) - 1) // RHS


def restrict_kernel(
    map_ref, fine_hbm, prol_hbm, op_hbm, rest_ref, prol, op, fine, wide, sums,
    field_sem, prol_sem, op_sem
):
    rows = fine.shape[0]
    sites = rows // SITES
    coarse = prol.shape[1]
    parts = 4
    size = rows // parts

    def field_copy(n):
        at = pl.ds(n * size, size)
        return pltpu.make_async_copy(fine_hbm.at[0, 0, at], fine.at[at], field_sem.at[n])

    def prol_copy(n):
        return pltpu.make_async_copy(prol_hbm.at[0, 0, n], prol.at[n], prol_sem.at[n])

    for n in range(parts):
        field_copy(n).start()
    for n in range(SITES):
        prol_copy(n).start()
    op_copy = pltpu.make_async_copy(op_hbm, op, op_sem)
    op_copy.start()
    for n in range(parts):
        field_copy(n).wait()

        def widen(index, carry):
            at = pl.ds(pl.multiple_of(n * size + index * 64, 64), 64)
            for g in range(3):
                wide[g, at, :] = fine[at, g * LANES:(g + 1) * LANES].astype(jnp.float32)
            return carry
        lax.fori_loop(0, size // 64, widen, 0)

    diagonal = lax.broadcasted_iota(jnp.int32, (8, LANES), 0) == lane_group((8, LANES))
    group = lane_group((coarse, LANES))

    def one_aggregate(agg, carry):
        prol_copy(agg).wait()

        def body(chunk, acc):
            parts = []
            for k in range(STEP):
                row = map_ref[0, 0, agg * sites + chunk * STEP + k]
                for g in range(3):
                    one = jnp.broadcast_to(wide[g, pl.ds(row, 1), :], (8, LANES))
                    parts.append(jnp.where(diagonal, one, 0.0))
            tiles = [
                jnp.concatenate(parts[i:i + 2], axis=0).astype(jnp.bfloat16)
                for i in range(0, len(parts), 2)
            ]
            spread = jnp.concatenate(tiles, axis=0)
            width = STEP * SPIN
            block = prol[agg, :, pl.ds(pl.multiple_of(chunk * width, width), width)]
            return acc + jnp.dot(block, spread, preferred_element_type=jnp.float32)

        sums[agg] = lax.fori_loop(
            0, sites // STEP, body, jnp.zeros((coarse, LANES), jnp.float32), unroll=True
        )
        return carry

    lax.fori_loop(0, SITES, one_aggregate, 0)
    packed = jnp.zeros((coarse, LANES), jnp.float32)
    for agg in range(SITES):
        acc = sums[agg]
        for shift in (16, 32, 64):
            acc = acc + pltpu.roll(acc, shift, 1)
        packed = jnp.where(group == agg, acc, packed)
    rest_ref[...] = packed.astype(jnp.bfloat16).astype(jnp.float32)
    op_copy.wait()


def richardson_kernel(
    nz, nt, rest_ref, op_ref, source, held, resid_ref, norm_ref,
    prol, deal, lines, packed, sent, halo, part, sums_z, sums_t,
    send_sem, recv_sem, zs_sem, zr_sem, ts_sem, tr_sem,
):
    z, t = lax.axis_index("gx"), lax.axis_index("ta")
    barrier = pltpu.get_barrier_semaphore()
    for d in range(1, nz):
        pl.semaphore_signal(barrier, inc=1, device_id=(lax.rem(z + d, nz), t), device_id_type=MESH)
    for d in range(1, nt):
        pl.semaphore_signal(barrier, inc=1, device_id=(z, lax.rem(t + d, nt)), device_id_type=MESH)

    rest = rest_ref[...]
    coarse = rest.shape[0]
    first = 0.5 * rest
    sent[0] = first.astype(jnp.bfloat16)

    targets = (
        (lax.rem(z + nz - 1, nz), t),
        (lax.rem(z + 1, nz), t),
        (z, lax.rem(t + nt - 1, nt)),
        (z, lax.rem(t + 1, nt)),
    )

    def exchange(turn):
        copies = []
        for slot, target in enumerate(targets):
            copy = pltpu.make_async_remote_copy(
                src_ref=sent.at[turn],
                dst_ref=halo.at[turn, pl.ds(slot * coarse, coarse)],
                send_sem=send_sem.at[turn, slot],
                recv_sem=recv_sem.at[turn, slot],
                device_id=target,
                device_id_type=MESH,
            )
            copy.start()
            copies.append(copy)
        return copies

    group = lane_group(rest.shape)
    even = lax.rem(group, 2) == 0

    def pick(full):
        result = full[0:coarse]
        for s in range(1, SITES):
            result = jnp.where(group == s, full[s * coarse:(s + 1) * coarse], result)
        return result

    depth = prol.shape[2]

    line = lax.broadcasted_iota(jnp.int32, (256, 256), 0)
    column = lax.broadcasted_iota(jnp.int32, (256, 256), 1)
    for u in range(4):
        turned = lax.rem(lax.rem(column, LANES) // 32 + (4 - u), 4)
        origin = 8 * lax.rem(column, 32) + 4 * (column // LANES) + turned
        deal[u] = (line == origin).astype(jnp.float32).astype(jnp.bfloat16)

    def deal_lanes(begin, end):
        def body(index, carry):
            for u in range(4):
                at = pl.ds(pl.multiple_of(index * 1024 + u * 256, 256), 256)
                block = source[:, :, at].reshape(SITES * coarse, 256)
                moved = jnp.dot(block, deal[u], preferred_element_type=jnp.float32)
                prol[:, :, at] = moved.astype(jnp.bfloat16).reshape(SITES, coarse, 256)
            return carry
        lax.fori_loop(begin, end, body, 0)

    pieces = depth // 1024

    def apply_blocks(values, turn, copies):
        up = pltpu.roll(values, LANES - YC * RHS, 1)
        down = pltpu.roll(values, YC * RHS, 1)
        swap = jnp.where(even, pltpu.roll(values, LANES - RHS, 1), pltpu.roll(values, RHS, 1))
        zero = jnp.zeros_like(values)
        stack = jnp.concatenate([values, up, down, swap, swap, zero], axis=0).astype(jnp.bfloat16)
        full = jnp.dot(packed[:, 4 * coarse:], stack, preferred_element_type=jnp.float32)
        near = pick(full)
        if turn == 0:
            deal_lanes(0, pieces // 2)
        for copy in copies:
            copy.wait()
        far = jnp.dot(packed[:, :4 * coarse], halo[turn], preferred_element_type=jnp.float32)
        return near + pick(far)

    for h in range(9):
        at = (h - 5 if h >= 5 else h + 4) * coarse
        for s in range(SITES):
            packed[s * coarse:(s + 1) * coarse, at:at + coarse] = op_ref[0, 0, s, h]
    packed[:, 9 * coarse:] = jnp.zeros((SITES * coarse, coarse), jnp.bfloat16)
    pl.semaphore_wait(barrier, nz - 1 + nt - 1)
    copies = exchange(0)
    first_resid = rest - apply_blocks(first, 0, copies)
    second_low = (first + 0.5 * first_resid).astype(jnp.bfloat16)
    sent[1] = second_low
    copies = exchange(1)
    second = second_low.astype(jnp.float32)
    resid = rest - apply_blocks(second, 1, copies)

    total = jnp.sum((resid * resid).reshape(coarse // 8, 8, LANES), axis=0)
    for shift in (16, 32, 64):
        total = total + pltpu.roll(total, shift, 1)
    part[0] = total

    def gather(turn, count, device, sums, s_sem, r_sem):
        pending = []
        for d in range(1, count):
            copy = pltpu.make_async_remote_copy(
                src_ref=part.at[turn],
                dst_ref=sums.at[d - 1],
                send_sem=s_sem.at[d - 1],
                recv_sem=r_sem.at[d - 1],
                device_id=device(d),
                device_id_type=MESH,
            )
            copy.start()
            pending.append(copy)
        return pending

    along_z = gather(0, nz, lambda d: (lax.rem(z + d, nz), t), sums_z, zs_sem, zr_sem)
    third = (second + 0.5 * resid).astype(jnp.bfloat16).astype(jnp.float32)
    lines[...] = jnp.transpose(third).astype(jnp.bfloat16)
    spot = lax.broadcasted_iota(jnp.int32, (RHS, LANES), 1) // 32
    quarter = lax.rem(lane_group((32, LANES)), 4)

    def lift(agg):
        left = lines[pl.ds(pl.multiple_of(agg * RHS, RHS), RHS), :]
        for b in range(pieces):
            flat = jnp.dot(
                left, prol[agg, :, b * 1024:(b + 1) * 1024], preferred_element_type=jnp.float32
            )
            stacked = []
            for i in range(8):
                half = i // 4 * LANES
                piece = flat[:, half:half + LANES]
                for u in range(1, 4):
                    other = flat[:, u * 256 + half:u * 256 + half + LANES]
                    piece = jnp.where(spot == (i + u) % 4, other, piece)
                stacked.append(piece)
            turned = jnp.transpose(jnp.concatenate(stacked, axis=0))
            for u in range(4):
                piece = turned[u * 32:(u + 1) * 32]
                for i in range(1, 4):
                    from_row = (i + u) % 4 * 32
                    piece = jnp.where(quarter == i, turned[from_row:from_row + 32], piece)
                at = agg * (depth // 8) + b * LANES + u * 32
                held[pl.ds(pl.multiple_of(at, 32), 32), :] = piece

    def lift_range(begin, end):
        def body(agg, carry):
            lift(agg)
            return carry
        lax.fori_loop(begin, end, body, 0, unroll=2)

    held[pl.ds(SITES * depth // 8, 8), :] = jnp.zeros((8, LANES), jnp.float32)
    deal_lanes(pieces // 2, pieces)
    for copy in along_z:
        copy.wait()
    for d in range(nz - 1):
        total = total + sums_z[d]
    part[1] = total
    along_t = gather(1, nt, lambda d: (z, lax.rem(t + d, nt)), sums_t, ts_sem, tr_sem)
    lift_range(0, SITES)
    resid_ref[...] = jnp.transpose(resid)
    for copy in along_t:
        copy.wait()
    for d in range(nt - 1):
        total = total + sums_t[d]
    norm_ref[...] = jnp.sqrt(jnp.sum(total, axis=0, keepdims=True) + 1e-06)


def place_kernel(
    map_ref, held, resid, norm, out_hbm, resid_ref, norm_ref, placed, out, out_sem
):
    rows = out.shape[0]
    norm_ref[...] = norm[:, :RHS]
    resid_ref[0, 0] = resid[...].reshape(resid_ref.shape[2:])

    def place(index, carry):
        for k in range(STEP):
            at = index * STEP + k
            row = map_ref[0, 0, at]
            placed[pl.ds(pl.multiple_of(row * 8, 8), 8), :] = held[pl.ds(3 * at, 8), :]
        return carry
    lax.fori_loop(0, rows // STEP, place, 0)

    def copy_out(n):
        at = pl.ds(pl.multiple_of(n * 256, 256), 256)
        return pltpu.make_async_copy(out.at[at], out_hbm.at[0, 0, at], out_sem.at[n])

    def narrow(index, carry):
        for g in range(3):
            out[pl.ds(pl.multiple_of(index * 256, 256), 256), g * LANES:(g + 1) * LANES] = (
                placed[pl.ds(index * 2048 + g, 256, stride=8), :].astype(jnp.bfloat16)
            )
        copy_out(index).start()
        return carry
    lax.fori_loop(0, rows // 256, narrow, 0)

    def finish(index, carry):
        copy_out(index).wait()
        return carry
    lax.fori_loop(0, rows // 256, finish, 0)


def local(nz, nt, fine_field, site_map, prolongator, coarse_op):
    rows, columns = fine_field.shape[2:]
    coarse, depth = prolongator.shape[3:]
    smem = pl.BlockSpec(memory_space=pltpu.SMEM)
    vmem = pl.BlockSpec(memory_space=pltpu.VMEM)
    hbm = pl.BlockSpec(memory_space=pltpu.HBM)
    dma = pltpu.SemaphoreType.DMA
    limit = 36 * 1024 * 1024

    restricted, held_prolongator, held_op = pl.pallas_call(
        restrict_kernel,
        out_shape=(
            pltpu.VMEM((coarse, LANES), jnp.float32),
            pltpu.VMEM((SITES, coarse, depth), jnp.bfloat16),
            pltpu.VMEM(coarse_op.shape, jnp.bfloat16),
        ),
        in_specs=[smem, hbm, hbm, hbm],
        out_specs=(vmem, vmem, vmem),
        scratch_shapes=[
            pltpu.VMEM((rows, columns), jnp.bfloat16),
            pltpu.VMEM((3, rows, LANES), jnp.float32),
            pltpu.VMEM((SITES, coarse, LANES), jnp.float32),
            dma((4,)),
            dma((SITES,)),
            dma(()),
        ],
        compiler_params=pltpu.CompilerParams(vmem_limit_bytes=56 * 1024 * 1024),
    )(site_map, fine_field, prolongator, coarse_op)

    held, packed_residual, norm = pl.pallas_call(
        functools.partial(richardson_kernel, nz, nt),
        out_shape=(
            pltpu.VMEM((rows * 3 + 8, LANES), jnp.float32),
            pltpu.VMEM((LANES, coarse), jnp.float32),
            pltpu.VMEM((1, LANES), jnp.float32),
        ),
        in_specs=[vmem, vmem, vmem],
        out_specs=(vmem, vmem, vmem),
        scratch_shapes=[
            pltpu.VMEM((SITES, coarse, depth), jnp.bfloat16),
            pltpu.VMEM((4, 256, 256), jnp.bfloat16),
            pltpu.VMEM((LANES, coarse), jnp.bfloat16),
            pltpu.VMEM((SITES * coarse, 10 * coarse), jnp.bfloat16),
            pltpu.VMEM((2, coarse, LANES), jnp.bfloat16),
            pltpu.VMEM((2, 4 * coarse, LANES), jnp.bfloat16),
            pltpu.VMEM((2, 8, LANES), jnp.float32),
            pltpu.VMEM((nz - 1, 8, LANES), jnp.float32),
            pltpu.VMEM((nt - 1, 8, LANES), jnp.float32),
            dma((2, 4)),
            dma((2, 4)),
            dma((nz - 1,)),
            dma((nz - 1,)),
            dma((nt - 1,)),
            dma((nt - 1,)),
        ],
        compiler_params=pltpu.CompilerParams(
            collective_id=0, has_side_effects=True, vmem_limit_bytes=limit
        ),
    )(restricted, held_op, held_prolongator)

    correction, coarse_residual, norm = pl.pallas_call(
        place_kernel,
        out_shape=(
            jax.ShapeDtypeStruct(fine_field.shape, fine_field.dtype),
            jax.ShapeDtypeStruct((1, 1, SITES, RHS, coarse), jnp.float32),
            jax.ShapeDtypeStruct((1, RHS), jnp.float32),
        ),
        in_specs=[smem, vmem, vmem, vmem],
        out_specs=(hbm, vmem, vmem),
        scratch_shapes=[
            pltpu.VMEM((rows * 8, LANES), jnp.float32),
            pltpu.VMEM((rows, columns), jnp.bfloat16),
            dma((rows // 256,)),
        ],
        compiler_params=pltpu.CompilerParams(vmem_limit_bytes=limit),
    )(site_map, held, packed_residual, norm)
    return (correction, jnp.swapaxes(coarse_residual, 3, 4), norm.reshape(RHS))


def solution(mesh):
    placed = (
        P("gx", "ta", None, None),
        P("gx", "ta", None),
        P("gx", "ta", None, None, None),
        P("gx", "ta", None, None, None, None),
    )
    return jax.shard_map(
        functools.partial(local, mesh.shape["gx"], mesh.shape["ta"]),
        mesh=mesh,
        in_specs=placed,
        out_specs=(P("gx", "ta", None, None), P("gx", "ta", None, None, None), P()),
        check_vma=False,
    )
```
